512 devices in a mesh: ctxa: 16 (over z, core), ctxb: 32 (over x, y).
Axes of the slice: x: 4, y: 8, z: 8, core: 2. Of those that a mesh axis runs over, the one named last changes fastest.
Arguments:
- queries: bfloat16 [131072, 8, 128], P(('ctxa', 'ctxb')), may hold values from -14 to 14
- key_vectors: bfloat16 [131072, 128], P(('ctxa', 'ctxb')), may hold values from -5 to 5
- value_vectors: bfloat16 [131072, 128], P(('ctxa', 'ctxb')), may hold values from -12 to 12
- out_grad: bfloat16 [131072, 8, 128], P(('ctxa', 'ctxb')), may hold values from -6 to 6
Outputs:
- attention: bfloat16 [131072, 8, 128], P(('ctxa', 'ctxb'))
- query_grad: bfloat16 [131072, 8, 128], P(('ctxa', 'ctxb'))
- key_grad: bfloat16 [131072, 128], P(('ctxa', 'ctxb'))
- value_grad: bfloat16 [131072, 128], P(('ctxa', 'ctxb'))
The draws below stay inside these ranges and needn't reach their ends.
All inputs are finite; a program needn't handle non-finite values.
Results may differ from the reference program's by a relative error of at most 0.012.
Values may be sent and summed in bfloat16 or wider, within the bound.
A program may use at most 64 MiB of HBM per device.

```python
import jax
import jax.numpy as jnp
from jax import lax

HQ = 8
DH = 128
BLK = 128
WIN = 1024
FAR = 6
TOKENS = 131072


def draw_queries(key, part):
    base_key = jax.random.fold_in(key, 11)
    return jnp.clip(2.0 * jax.random.normal(base_key, (TOKENS, HQ, DH), jnp.float32), -10.0, 10.0).astype(jnp.bfloat16)


def draw_key_vectors(key, part):
    base_key = jax.random.fold_in(key, 13)
    return jnp.clip(jax.random.normal(base_key, (TOKENS, DH), jnp.float32), -5.0, 5.0).astype(jnp.bfloat16)


def shard_levels(own_key, shape, cuts, low, top_value):
    def one(dim, parts):
        steps = jax.random.uniform(jax.random.fold_in(jax.random.fold_in(own_key, 6), dim), (parts,), jnp.float32, low / len(cuts), top_value / len(cuts))
        return jnp.repeat(jnp.exp(steps), shape[dim] // parts).reshape((-1,) + (1,) * (len(shape) - dim - 1))

    gain = one(*cuts[0])
    for cut in cuts[1:]:
        gain = gain * one(*cut)
    return gain


def normal_values(own_key, shape, spread, limit, pieces=(), kind=jnp.bfloat16):
    drawn = spread * jax.random.normal(own_key, shape, jnp.float32)
    if pieces:
        drawn = drawn * shard_levels(own_key, shape, pieces, -0.22, 0.18)
    return jnp.clip(drawn, -limit, limit).astype(kind)


def setup_inputs(seed: int = 0) -> dict:
    seeds = jax.random.split(jax.random.key(seed), 5)
    return {
        "queries": draw_queries(jax.random.fold_in(seeds[4], 71), 0),
        "key_vectors": draw_key_vectors(jax.random.fold_in(seeds[4], 71), 0),
        "value_vectors": normal_values(seeds[2], (TOKENS, DH), 2.0, 12.0, ((0, 512),)),
        "out_grad": normal_values(seeds[3], (TOKENS, HQ, DH), 1.0, 6.0, ((0, 512),)),
    }


def reference(queries, key_vectors, value_vectors, out_grad):
    score_scale = 1.0 / (DH ** 0.5)
    stride = 2 * WIN // BLK
    key_span = WIN + BLK
    row_count = BLK * HQ
    total_keys = key_span + FAR * BLK
    offsets = jnp.arange(key_span, dtype=jnp.int32)
    inside = jnp.arange(BLK, dtype=jnp.int32)
    block_count = TOKENS // BLK

    def one_block(running, block_index):
        block_start = (block_index * BLK).astype(jnp.int32)
        q_rows = lax.dynamic_slice_in_dim(queries, block_start, BLK, 0).reshape(row_count, DH)
        grad_rows = lax.dynamic_slice_in_dim(out_grad, block_start, BLK, 0).reshape(row_count, DH)
        near_start = jnp.maximum(block_start - WIN, 0).astype(jnp.int32)
        q_pos = block_start + inside
        k_pos = near_start + offsets
        starts = [near_start]
        lengths = [key_span]
        masks = [(k_pos[None, :] > q_pos[:, None] - WIN) & (k_pos[None, :] <= q_pos[:, None])]
        for level_index in range(FAR):
            far_block = block_index - stride * (2 ** level_index)
            starts.append((jnp.maximum(far_block, 0) * BLK).astype(jnp.int32))
            lengths.append(BLK)
            masks.append(jnp.broadcast_to(far_block >= 0, (BLK, BLK)))
        key_rows = jnp.concatenate([lax.dynamic_slice_in_dim(key_vectors, begin, size, 0) for begin, size in zip(starts, lengths)], axis=0)
        value_rows = jnp.concatenate([lax.dynamic_slice_in_dim(value_vectors, begin, size, 0) for begin, size in zip(starts, lengths)], axis=0)
        visible = jnp.concatenate(masks, axis=1)
        visible = jnp.broadcast_to(visible[:, None, :], (BLK, HQ, total_keys)).reshape(row_count, total_keys)
        scores = jnp.einsum("rd,kd->rk", q_rows.astype(jnp.float32), key_rows.astype(jnp.float32)) * score_scale
        scores = jnp.where(visible, scores, -jnp.inf)
        row_max = jnp.max(scores, axis=1, keepdims=True)
        log_total = row_max + jnp.log(jnp.sum(jnp.exp(scores - row_max), axis=1, keepdims=True))
        probs = jnp.exp(scores - log_total)
        probs_low = probs.astype(jnp.bfloat16)
        out_rows = jnp.dot(probs_low, value_rows, preferred_element_type=jnp.float32).astype(jnp.bfloat16)
        row_delta = jnp.sum(grad_rows.astype(jnp.float32) * out_rows.astype(jnp.float32), axis=1, keepdims=True)
        prob_grad = jnp.einsum("rd,kd->rk", grad_rows.astype(jnp.float32), value_rows.astype(jnp.float32))
        score_grad = (probs * (prob_grad - row_delta)).astype(jnp.bfloat16)
        q_grad_rows = (jnp.dot(score_grad, key_rows, preferred_element_type=jnp.float32) * score_scale).astype(jnp.bfloat16)
        key_terms = jnp.einsum("rk,rd->kd", score_grad.astype(jnp.float32), q_rows.astype(jnp.float32)) * score_scale
        value_terms = jnp.einsum("rk,rd->kd", probs_low.astype(jnp.float32), grad_rows.astype(jnp.float32))
        grad_terms = jnp.stack([key_terms, value_terms])
        position = 0
        for begin, size in zip(starts, lengths):
            previous = lax.dynamic_slice_in_dim(running, begin, size, 1)
            running = lax.dynamic_update_slice_in_dim(running, previous + grad_terms[:, position:position + size], begin, 1)
            position = position + size
        return running, (out_rows.reshape(BLK, HQ, DH), q_grad_rows.reshape(BLK, HQ, DH))

    running = jnp.zeros((2, TOKENS, DH), jnp.float32)
    running, outputs = lax.scan(one_block, running, jnp.arange(block_count, dtype=jnp.int32))
    attention = outputs[0].reshape(TOKENS, HQ, DH)
    query_grad = outputs[1].reshape(TOKENS, HQ, DH)
    return attention, query_grad, running[0].astype(jnp.bfloat16), running[1].astype(jnp.bfloat16)
```

```python
import functools

import jax
import jax.numpy as jnp
from jax import lax
from jax.experimental import pallas as pl
from jax.experimental.pallas import tpu as pltpu
from jax.sharding import PartitionSpec as P

BLK = 128
F32 = jnp.float32
BF16 = jnp.bfloat16
MESH = pl.DeviceIdType.MESH
NEG = -1e30
NT = (((1,), (1,)), ((), ()))
NN = (((1,), (0,)), ((), ()))

DISTS = (1, 2, 3, 4, 8, 16, 32, 64, 128, 256)
SLOT = {d: i for i, d in enumerate(DISTS)}
PAIRS = ((8, 16), (64, 32), (128, 256))
OWN = 4
GROUPS = 8


def dot(a, b, dims):
    return lax.dot_general(a, b, dims, preferred_element_type=F32)


def kernel(
    inner, total, q, do, k, v, out, dq, dk, dv,
    win, far, score, prob, top, inv, dlow, qt, dt, delta, term, got, own,
    fsend, frecv, bsend, brecv,
):
    me = lax.axis_index("ctxa") * inner + lax.axis_index("ctxb")
    core = (me // inner) % 2
    scale = 1.0 / BLK**0.5
    unit = scale * 1.4426950408889634

    def place(delta_):
        return ((me + delta_) // inner, (me + delta_) % inner)

    mate = inner * (1 - 2 * core)

    def exists(delta_):
        return (me + delta_ >= 0) & (me + delta_ < total)

    barrier = pltpu.get_barrier_semaphore()
    count = jnp.int32(1)
    pl.semaphore_signal(barrier, inc=1, device_id=place(mate), device_id_type=MESH)
    for step in (1, -1, 8, -8, 64, -64, 128, -128):
        ok = exists(step)

        @pl.when(ok)
        def _(step=step):
            pl.semaphore_signal(barrier, inc=1, device_id=place(step), device_id_type=MESH)

        count = count + ok.astype(jnp.int32)
    pl.semaphore_wait(barrier, count)

    def held(kind, dist):
        if dist == 0:
            return k if kind == 0 else v
        if dist <= 4:
            return win.at[kind, dist - 1]
        for i, pair in enumerate(PAIRS):
            if dist in pair:
                return far.at[kind, i, :, pair.index(dist)]

    forward = [
        (0, 64, 64), (0, 1, 1), (0, 8, 8), (64, 64, 128), (1, 1, 2), (8, 8, 16),
        (128, 128, 256), (2, 1, 3), (3, 1, 4), (0, 32, 32), (64, -32, 32),
    ]

    def forward_ok(item):
        source, step, _ = item
        ok = (me - source >= 0) & exists(step)
        if step == 32:
            ok = core == 0
        if step == -32:
            ok = ok & (core == 1)
        return ok

    def forward_copy(kind, i):
        source, step, target = forward[i]
        return pltpu.make_async_remote_copy(
            src_ref=held(kind, source),
            dst_ref=held(kind, target),
            send_sem=fsend.at[kind, i],
            recv_sem=frecv.at[kind, SLOT[target]],
            device_id=place(step),
            device_id_type=MESH,
        )

    def pass_on(kind, dist):
        for i, item in enumerate(forward):
            if item[0] == dist:

                @pl.when(forward_ok(item))
                def _(i=i):
                    forward_copy(kind, i).start()

    def arrive(kind, dist):
        i = [item[2] for item in forward].index(dist)

        @pl.when(me >= dist)
        def _():
            forward_copy(kind, i).wait_recv()

        pass_on(kind, dist)

    for kind in range(2):
        pass_on(kind, 0)

    for dist in DISTS:

        @pl.when(me < dist)
        def _(dist=dist):
            for kind in range(2):
                ref = held(kind, dist)
                ref[...] = jnp.zeros(ref.shape, BF16)

    def operand(kind, group, b):
        if group == OWN:
            value = (k if kind == 0 else v)[...]
        elif group < OWN:
            value = win[kind, group]
        else:
            value = far[kind, group - OWN - 1, b]
        return value.reshape(2 * BLK, BLK)

    def scores(group):
        def body(b, _):
            keys = operand(0, group, b)
            for c in range(4):
                rows = pl.ds(c * 256, 256)
                s = dot(q[b, rows, :], keys, NT)
                if group == OWN or group == 3:
                    tok = b * BLK + (c * 256 + lax.broadcasted_iota(jnp.int32, (256, 256), 0)) // 8
                    col = lax.broadcasted_iota(jnp.int32, (256, 256), 1)
                    seen = col <= tok if group == OWN else (col > tok) & (me >= 4)
                    s = jnp.where(seen, s, NEG)
                    s0, s1 = s[:, :BLK], s[:, BLK:]
                else:
                    pair = (group + 1,) * 2 if group < OWN else PAIRS[group - OWN - 1]
                    s0 = jnp.where(me >= pair[0], s[:, :BLK], NEG)
                    s1 = jnp.where(me >= pair[1], s[:, BLK:], NEG)
                score[b, group, rows, :BLK] = s0
                score[b, group, rows, BLK:] = s1
                most = jnp.maximum(s0, s1)
                if group != OWN:
                    most = jnp.maximum(most, top[b, rows, :])
                top[b, rows, :] = most
            return 0

        lax.fori_loop(0, 2, body, 0)

    for b in range(2):
        for c in range(8):
            qt[b, :, c * BLK : (c + 1) * BLK] = q[b, c * BLK : (c + 1) * BLK, :].T
    scores(OWN)
    for dist in (1, 8, 64):
        arrive(0, dist)
    scores(0)
    for dist in (1, 8, 64):
        arrive(1, dist)
    for dist in (2, 16, 128):
        arrive(0, dist)
    scores(1)
    scores(5)
    for dist in (2, 16, 128):
        arrive(1, dist)
    arrive(0, 3)
    scores(2)
    arrive(1, 3)
    arrive(0, 32)
    scores(6)
    arrive(0, 4)
    scores(3)
    arrive(0, 256)
    scores(7)

    def soften(i, _):
        b = i // 8
        start = pl.multiple_of((i % 8) * BLK, BLK)
        rows = pl.ds(start, BLK)
        most = jnp.max(top[b, rows, :], axis=1, keepdims=True) * unit
        most = jnp.broadcast_to(most, (BLK, BLK))
        sums = jnp.zeros((BLK, BLK), F32)
        for group in range(GROUPS):
            for h in range(2):
                lanes = slice(h * BLK, (h + 1) * BLK)
                e = jnp.exp2(score[b, group, rows, lanes] * unit - most)
                sums = sums + e
                prob[b, group, rows, lanes] = e.astype(BF16)
        part = jnp.broadcast_to(1.0 / jnp.sum(sums, axis=1, keepdims=True), (BLK, BLK))
        inv[b, rows, :] = part
        low = (do[b, rows, :].astype(F32) * part).astype(BF16)
        dlow[b, rows, :] = low
        dt[b, :, rows] = low.T
        return 0

    lax.fori_loop(0, 16, soften, 0)

    back = [
        (256, -128, ()), (4, -1, ()), (16, -8, ()), (128, -64, (256,)), (3, -1, (4,)),
        (8, -8, (16,)), (64, -64, (128, 32)), (2, -1, (3,)), (1, -1, (2,)), (32, 0, ()),
    ]
    back_index = {item[0]: i for i, item in enumerate(back)}
    back_step = {item[0]: -item[1] for item in back}

    def back_copy(kind, dist):
        i = back_index[dist]
        step = back[i][1] if dist != 32 else mate
        return pltpu.make_async_remote_copy(
            src_ref=term.at[kind, SLOT[dist]],
            dst_ref=got.at[kind, SLOT[dist]],
            send_sem=bsend.at[kind, i],
            recv_sem=brecv.at[kind, SLOT[dist]],
            device_id=place(step),
            device_id_type=MESH,
        )

    def send_back(kind, dist):
        mine = SLOT[dist]
        for other in back[back_index[dist]][2]:
            if other == 32:
                ok = (me >= dist) & (core == 1)
            else:
                ok = (me >= dist) & exists(back_step[other])

            @pl.when(ok)
            def _(other=other):
                back_copy(kind, other).wait_recv()
                term[kind, mine] = (
                    term[kind, mine].astype(F32) + got[kind, SLOT[other]].astype(F32)
                ).astype(BF16)

        @pl.when(me >= dist)
        def _():
            back_copy(kind, dist).start()

    def reduce_rows(kind, group, left, factor):
        if group <= OWN:
            r = dot(left[0], prob[0, group], NN) + dot(left[1], prob[1, group], NN)
            if group == OWN:
                own[kind] = r * factor
            else:
                term[kind, group] = (r * factor).astype(BF16)
        else:
            pair = PAIRS[group - OWN - 1]
            for b in range(2):
                r = (dot(left[b], prob[b, group], NN) * factor).astype(BF16)
                for h in range(2):
                    term[kind, SLOT[pair[h]], :, b * BLK : (b + 1) * BLK] = r[
                        :, h * BLK : (h + 1) * BLK
                    ]

    reduce_rows(1, 7, dt, 1.0)
    send_back(1, 256)
    reduce_rows(1, 3, dt, 1.0)
    send_back(1, 4)
    reduce_rows(1, 5, dt, 1.0)
    send_back(1, 16)
    reduce_rows(1, 6, dt, 1.0)
    send_back(1, 32)
    reduce_rows(1, 2, dt, 1.0)
    reduce_rows(1, 1, dt, 1.0)
    send_back(1, 3)
    reduce_rows(1, 0, dt, 1.0)
    reduce_rows(1, OWN, dt, 1.0)
    send_back(1, 128)
    send_back(1, 8)

    for dist in (32, 4, 256):
        arrive(1, dist)

    def attend(i, _):
        b = i // 4
        rows = pl.ds(pl.multiple_of((i % 4) * 256, 256), 256)
        acc = dot(prob[b, 0, rows, :], operand(1, 0, b), NN)
        for group in range(1, GROUPS):
            acc = acc + dot(prob[b, group, rows, :], operand(1, group, b), NN)
        low = (acc * inv[b, rows, :]).astype(BF16)
        out[b, rows, :] = low
        d = jnp.sum(dlow[b, rows, :].astype(F32) * low.astype(F32), axis=1, keepdims=True)
        delta[b, rows, :] = jnp.broadcast_to(d, (256, BLK))
        return 0

    lax.fori_loop(0, 8, attend, 0, unroll=2)
    send_back(1, 2)

    def score_grads(group):
        def body(b, _):
            values = operand(1, group, b)
            for c in range(4):
                rows = pl.ds(c * 256, 256)
                dp = dot(dlow[b, rows, :], values, NT)
                d = delta[b, rows, :]
                for h in range(2):
                    lanes = slice(h * BLK, (h + 1) * BLK)
                    p = prob[b, group, rows, lanes].astype(F32)
                    prob[b, group, rows, lanes] = (p * (dp[:, lanes] - d)).astype(BF16)
            return 0

        lax.fori_loop(0, 2, body, 0)
        reduce_rows(0, group, qt, scale)

    score_grads(7)
    send_back(0, 256)
    send_back(1, 64)
    score_grads(3)
    send_back(0, 4)
    send_back(1, 1)
    score_grads(5)
    send_back(0, 16)
    score_grads(6)
    send_back(0, 32)
    score_grads(2)
    send_back(0, 3)
    send_back(0, 128)
    score_grads(1)
    send_back(0, 2)
    send_back(0, 8)
    score_grads(0)
    send_back(0, 64)
    send_back(0, 1)
    score_grads(OWN)

    def query_grads(i, _):
        b = i // 4
        rows = pl.ds(pl.multiple_of((i % 4) * 256, 256), 256)
        acc = dot(prob[b, 0, rows, :], operand(0, 0, b), NN)
        for group in range(1, GROUPS):
            acc = acc + dot(prob[b, group, rows, :], operand(0, group, b), NN)
        dq[b, rows, :] = (acc * scale).astype(BF16)
        return 0

    lax.fori_loop(0, 8, query_grads, 0, unroll=2)

    for kind, result in ((1, dv), (0, dk)):
        for dist in (1, 8, 64, 32):
            ok = (core == 0) if dist == 32 else exists(dist)

            @pl.when(ok)
            def _(kind=kind, dist=dist):
                back_copy(kind, dist).wait_recv()
                own[kind] = own[kind] + got[kind, SLOT[dist]].astype(F32)

        result[...] = own[kind].T.astype(BF16)

    for kind in range(2):
        for i, item in enumerate(forward):

            @pl.when(forward_ok(item))
            def _(kind=kind, i=i):
                forward_copy(kind, i).wait_send()

        for dist in DISTS:

            @pl.when(me >= dist)
            def _(kind=kind, dist=dist):
                back_copy(kind, dist).wait_send()


def solution(mesh):
    inner = mesh.shape["ctxb"]
    total = mesh.shape["ctxa"] * inner

    def body(queries, key_vectors, value_vectors, out_grad):
        toks, heads, width = queries.shape
        rows = toks * heads // 2
        big = (2, rows, width)
        vmem = pl.BlockSpec(memory_space=pltpu.VMEM)
        attention, query_grad, key_grad, value_grad = pl.pallas_call(
            functools.partial(kernel, inner, total),
            out_shape=(
                jax.ShapeDtypeStruct(big, BF16),
                jax.ShapeDtypeStruct(big, BF16),
                jax.ShapeDtypeStruct((toks, width), BF16),
                jax.ShapeDtypeStruct((toks, width), BF16),
            ),
            in_specs=[vmem] * 4,
            out_specs=[vmem] * 4,
            scratch_shapes=[
                pltpu.VMEM((2, 4, 2, BLK, width), BF16),
                pltpu.VMEM((2, 3, 2, 2, BLK, width), BF16),
                pltpu.VMEM((2, GROUPS, rows, 2 * BLK), F32),
                pltpu.VMEM((2, GROUPS, rows, 2 * BLK), BF16),
                pltpu.VMEM(big, F32),
                pltpu.VMEM(big, F32),
                pltpu.VMEM(big, BF16),
                pltpu.VMEM((2, width, rows), BF16),
                pltpu.VMEM((2, width, rows), BF16),
                pltpu.VMEM(big, F32),
                pltpu.VMEM((2, 10, width, 2 * BLK), BF16),
                pltpu.VMEM((2, 10, width, 2 * BLK), BF16),
                pltpu.VMEM((2, width, 2 * BLK), F32),
                pltpu.SemaphoreType.DMA((2, 11)),
                pltpu.SemaphoreType.DMA((2, 10)),
                pltpu.SemaphoreType.DMA((2, 10)),
                pltpu.SemaphoreType.DMA((2, 10)),
            ],
            compiler_params=pltpu.CompilerParams(
                collective_id=0, has_side_effects=True, vmem_limit_bytes=56 * 2**20
            ),
        )(
            queries.reshape(big),
            out_grad.reshape(big),
            key_vectors.reshape(2, BLK, width),
            value_vectors.reshape(2, BLK, width),
        )
        return (
            attention.reshape(queries.shape),
            query_grad.reshape(queries.shape),
            key_grad,
            value_grad,
        )

    tokens = P(("ctxa", "ctxb"), None)
    rows = P(("ctxa", "ctxb"), None, None)
    return jax.shard_map(
        body,
        mesh=mesh,
        in_specs=(rows, tokens, tokens, rows),
        out_specs=(rows, rows, tokens, tokens),
        check_vma=False,
    )
```

```python
import functools

import jax
import jax.numpy as jnp
from jax import lax
from jax.experimental import pallas as pl
from jax.experimental.pallas import tpu as pltpu
from jax.sharding import PartitionSpec as P

BLK = 128
F32 = jnp.float32
BF16 = jnp.bfloat16
MESH = pl.DeviceIdType.MESH
NEG = -1e30
NT = (((1,), (1,)), ((), ()))
NN = (((1,), (0,)), ((), ()))

DISTS = (1, 2, 3, 4, 8, 16, 32, 64, 128, 256)
SLOT = {d: i for i, d in enumerate(DISTS)}
PAIRS = ((8, 16), (64, 32), (128, 256))
OWN = 4
GROUPS = 8


def dot(a, b, dims):
    return lax.dot_general(a, b, dims, preferred_element_type=F32)


def kernel(
    inner, total, q, do, k, v, out, dq, dk, dv,
    win, far, score, prob, top, inv, dlow, qt, dt, delta, term, got, own,
    fsend, frecv, bsend, brecv,
):
    me = lax.axis_index("ctxa") * inner + lax.axis_index("ctxb")
    core = (me // inner) % 2
    scale = 1.0 / BLK**0.5
    unit = scale * 1.4426950408889634

    def place(delta_):
        return ((me + delta_) // inner, (me + delta_) % inner)

    mate = inner * (1 - 2 * core)

    def exists(delta_):
        return (me + delta_ >= 0) & (me + delta_ < total)

    barrier = pltpu.get_barrier_semaphore()
    count = jnp.int32(1)
    pl.semaphore_signal(barrier, inc=1, device_id=place(mate), device_id_type=MESH)
    for step in (2, -2, 128, -128, 64, -64, 1, -1, 8, -8, 16, -16):
        ok = exists(step)

        @pl.when(ok)
        def _(step=step):
            pl.semaphore_signal(barrier, inc=1, device_id=place(step), device_id_type=MESH)

        count = count + ok.astype(jnp.int32)
    pl.semaphore_wait(barrier, count)

    def held(kind, dist):
        if dist == 0:
            return k if kind == 0 else v
        if dist <= 4:
            return win.at[kind, dist - 1]
        for i, pair in enumerate(PAIRS):
            if dist in pair:
                return far.at[kind, i, :, pair.index(dist)]

    forward = [
        (0, 2, 2), (0, 128, 128), (0, 64, 64), (0, 1, 1), (0, 8, 8), (0, 16, 16), (0, 32, 32),
        (2, 2, 4), (2, 1, 3), (128, 128, 256), (64, -32, 32),
    ]

    def forward_ok(item):
        source, step, _ = item
        ok = (me - source >= 0) & exists(step)
        if step == 32:
            ok = core == 0
        if step == -32:
            ok = ok & (core == 1)
        return ok

    def forward_copy(kind, i):
        source, step, target = forward[i]
        return pltpu.make_async_remote_copy(
            src_ref=held(kind, source),
            dst_ref=held(kind, target),
            send_sem=fsend.at[kind, i],
            recv_sem=frecv.at[kind, SLOT[target]],
            device_id=place(step),
            device_id_type=MESH,
        )

    def pass_on(kind, dist):
        for i, item in enumerate(forward):
            if item[0] == dist:

                @pl.when(forward_ok(item))
                def _(i=i):
                    forward_copy(kind, i).start()

    def arrive(kind, dist):
        i = [item[2] for item in forward].index(dist)

        @pl.when(me >= dist)
        def _():
            forward_copy(kind, i).wait_recv()

        pass_on(kind, dist)

    pass_on(0, 0)

    for dist in DISTS:

        @pl.when(me < dist)
        def _(dist=dist):
            for kind in range(2):
                ref = held(kind, dist)
                ref[...] = jnp.zeros(ref.shape, BF16)

    def operand(kind, group, b):
        if group == OWN:
            value = (k if kind == 0 else v)[...]
        elif group < OWN:
            value = win[kind, group]
        else:
            value = far[kind, group - OWN - 1, b]
        return value.reshape(2 * BLK, BLK)

    def scores(group):
        def body(b, _):
            keys = operand(0, group, b)
            for c in range(4):
                rows = pl.ds(c * 256, 256)
                s = dot(q[b, rows, :], keys, NT) * unit
                if group == OWN or group == 3:
                    tok = b * BLK + (c * 256 + lax.broadcasted_iota(jnp.int32, (256, 256), 0)) // 8
                    col = lax.broadcasted_iota(jnp.int32, (256, 256), 1)
                    seen = col <= tok if group == OWN else (col > tok) & (me >= 4)
                    s = jnp.where(seen, s, NEG)
                    s0, s1 = s[:, :BLK], s[:, BLK:]
                else:
                    pair = (group + 1,) * 2 if group < OWN else PAIRS[group - OWN - 1]
                    s0 = jnp.where(me >= pair[0], s[:, :BLK], NEG)
                    s1 = jnp.where(me >= pair[1], s[:, BLK:], NEG)
                score[b, group, rows, :BLK] = s0
                score[b, group, rows, BLK:] = s1
                most = jnp.maximum(s0, s1)
                if group != OWN:
                    most = jnp.maximum(most, top[b, rows, :])
                top[b, rows, :] = most
            return 0

        lax.fori_loop(0, 2, body, 0)

    for b in range(2):
        for c in range(8):
            qt[b, :, c * BLK : (c + 1) * BLK] = q[b, c * BLK : (c + 1) * BLK, :].T
    scores(OWN)
    for dist in (2, 128, 64):
        arrive(0, dist)
    pass_on(1, 0)
    arrive(0, 1)
    scores(0)
    scores(1)
    for dist in (8, 16):
        arrive(0, dist)
    scores(5)
    for dist in (2, 128, 64):
        arrive(1, dist)
    arrive(0, 3)
    scores(2)
    arrive(0, 32)
    scores(6)
    arrive(0, 4)
    scores(3)
    arrive(0, 256)
    scores(7)

    def soften(i, _):
        b = i // 8
        start = pl.multiple_of((i % 8) * BLK, BLK)
        rows = pl.ds(start, BLK)
        most = jnp.max(top[b, rows, :], axis=1, keepdims=True)
        most = jnp.broadcast_to(most, (BLK, BLK))
        sums = [jnp.zeros((BLK, BLK), F32)] * 2
        for group in range(GROUPS):
            for h in range(2):
                lanes = slice(h * BLK, (h + 1) * BLK)
                e = jnp.exp2(score[b, group, rows, lanes] - most)
                sums[h] = sums[h] + e
                prob[b, group, rows, lanes] = e.astype(BF16)
        part = 1.0 / jnp.sum(sums[0] + sums[1], axis=1, keepdims=True)
        part = jnp.broadcast_to(part, (BLK, BLK))
        inv[b, rows, :] = part
        low = (do[b, rows, :].astype(F32) * part).astype(BF16)
        dlow[b, rows, :] = low
        dt[b, :, rows] = low.T
        return 0

    lax.fori_loop(0, 16, soften, 0, unroll=4)

    back = [
        (4, -2, ()), (3, -1, ()), (256, -128, ()), (32, 0, ()), (16, -16, ()), (8, -8, ()),
        (1, -1, ()), (2, -2, (4, 3)), (128, -128, (256,)), (64, -64, (32,)),
    ]
    back_index = {item[0]: i for i, item in enumerate(back)}
    back_step = {item[0]: -item[1] for item in back}

    def back_copy(kind, dist):
        i = back_index[dist]
        step = back[i][1] if dist != 32 else mate
        return pltpu.make_async_remote_copy(
            src_ref=term.at[kind, SLOT[dist]],
            dst_ref=got.at[kind, SLOT[dist]],
            send_sem=bsend.at[kind, i],
            recv_sem=brecv.at[kind, SLOT[dist]],
            device_id=place(step),
            device_id_type=MESH,
        )

    def send_back(kind, dist):
        mine = SLOT[dist]
        for other in back[back_index[dist]][2]:
            if other == 32:
                ok = (me >= dist) & (core == 1)
            else:
                ok = (me >= dist) & exists(back_step[other])

            @pl.when(ok)
            def _(other=other):
                back_copy(kind, other).wait_recv()
                term[kind, mine] = (
                    term[kind, mine].astype(F32) + got[kind, SLOT[other]].astype(F32)
                ).astype(BF16)

        @pl.when(me >= dist)
        def _():
            back_copy(kind, dist).start()

    def reduce_rows(kind, group, left, factor):
        if group <= OWN:
            r = dot(left[0], prob[0, group], NN) + dot(left[1], prob[1, group], NN)
            if group == OWN:
                own[kind] = r * factor
            else:
                term[kind, group] = (r * factor).astype(BF16)
        else:
            pair = PAIRS[group - OWN - 1]
            for b in range(2):
                r = (dot(left[b], prob[b, group], NN) * factor).astype(BF16)
                for h in range(2):
                    term[kind, SLOT[pair[h]], :, b * BLK : (b + 1) * BLK] = r[
                        :, h * BLK : (h + 1) * BLK
                    ]

    order = (
        (3, (4,)), (2, (3,)), (7, (256,)), (6, (32,)), (5, (16, 8)), (1, ()), (0, (1,)), (OWN, ()),
    )
    for group, dists in order:
        reduce_rows(1, group, dt, 1.0)
        for dist in dists:
            send_back(1, dist)
    for dist in (1, 8, 16, 3, 4, 32, 256):
        arrive(1, dist)

    def attend(i, _):
        b = i // 4
        rows = pl.ds(pl.multiple_of((i % 4) * 256, 256), 256)
        acc = dot(prob[b, 0, rows, :], operand(1, 0, b), NN)
        for group in range(1, GROUPS):
            acc = acc + dot(prob[b, group, rows, :], operand(1, group, b), NN)
        low = (acc * inv[b, rows, :]).astype(BF16)
        out[b, rows, :] = low
        d = jnp.sum(dlow[b, rows, :].astype(F32) * low.astype(F32), axis=1, keepdims=True)
        delta[b, rows, :] = jnp.broadcast_to(d, (256, BLK))
        return 0

    lax.fori_loop(0, 8, attend, 0, unroll=4)
    for dist in (2, 128, 64):
        send_back(1, dist)

    def score_grads(group):
        def body(b, _):
            values = operand(1, group, b)
            for c in range(4):
                rows = pl.ds(c * 256, 256)
                dp = dot(dlow[b, rows, :], values, NT)
                d = delta[b, rows, :]
                for h in range(2):
                    lanes = slice(h * BLK, (h + 1) * BLK)
                    p = prob[b, group, rows, lanes].astype(F32)
                    prob[b, group, rows, lanes] = (p * (dp[:, lanes] - d)).astype(BF16)
            return 0

        lax.fori_loop(0, 2, body, 0)
        reduce_rows(0, group, qt, scale)

    for group, dists in order:
        score_grads(group)
        for dist in dists:
            send_back(0, dist)
        if group == 0:
            for dist in (2, 128, 64):
                send_back(0, dist)

    def query_grads(i, _):
        b = i // 4
        rows = pl.ds(pl.multiple_of((i % 4) * 256, 256), 256)
        acc = dot(prob[b, 0, rows, :], operand(0, 0, b), NN)
        for group in range(1, GROUPS):
            acc = acc + dot(prob[b, group, rows, :], operand(0, group, b), NN)
        dq[b, rows, :] = (acc * scale).astype(BF16)
        return 0

    lax.fori_loop(0, 8, query_grads, 0, unroll=4)

    for kind, result in ((1, dv), (0, dk)):
        for dist in (1, 8, 16, 2, 128, 64, 32):
            ok = (core == 0) if dist == 32 else exists(dist)

            @pl.when(ok)
            def _(kind=kind, dist=dist):
                back_copy(kind, dist).wait_recv()
                own[kind] = own[kind] + got[kind, SLOT[dist]].astype(F32)

        result[...] = own[kind].T.astype(BF16)

    for kind in range(2):
        for i, item in enumerate(forward):

            @pl.when(forward_ok(item))
            def _(kind=kind, i=i):
                forward_copy(kind, i).wait_send()

        for dist in DISTS:

            @pl.when(me >= dist)
            def _(kind=kind, dist=dist):
                back_copy(kind, dist).wait_send()


def hand_over(*refs):
    copies = [pltpu.make_async_copy(refs[i], refs[4 + i], refs[8].at[i]) for i in range(4)]
    for copy in copies:
        copy.start()
    for copy in copies:
        copy.wait()


def solution(mesh):
    inner = mesh.shape["ctxb"]
    total = mesh.shape["ctxa"] * inner

    def body(queries, key_vectors, value_vectors, out_grad):
        toks, heads, width = queries.shape
        rows = toks * heads // 2
        big = (2, rows, width)
        vmem = pl.BlockSpec(memory_space=pltpu.VMEM)
        shapes = (
            jax.ShapeDtypeStruct(big, BF16),
            jax.ShapeDtypeStruct(big, BF16),
            jax.ShapeDtypeStruct((toks, width), BF16),
            jax.ShapeDtypeStruct((toks, width), BF16),
        )
        results = pl.pallas_call(
            functools.partial(kernel, inner, total),
            out_shape=shapes,
            in_specs=[vmem] * 4,
            out_specs=[vmem] * 4,
            scratch_shapes=[
                pltpu.VMEM((2, 4, 2, BLK, width), BF16),
                pltpu.VMEM((2, 3, 2, 2, BLK, width), BF16),
                pltpu.VMEM((2, GROUPS, rows, 2 * BLK), F32),
                pltpu.VMEM((2, GROUPS, rows, 2 * BLK), BF16),
                pltpu.VMEM(big, F32),
                pltpu.VMEM(big, F32),
                pltpu.VMEM(big, BF16),
                pltpu.VMEM((2, width, rows), BF16),
                pltpu.VMEM((2, width, rows), BF16),
                pltpu.VMEM(big, F32),
                pltpu.VMEM((2, 10, width, 2 * BLK), BF16),
                pltpu.VMEM((2, 10, width, 2 * BLK), BF16),
                pltpu.VMEM((2, width, 2 * BLK), F32),
                pltpu.SemaphoreType.DMA((2, 11)),
                pltpu.SemaphoreType.DMA((2, 10)),
                pltpu.SemaphoreType.DMA((2, 10)),
                pltpu.SemaphoreType.DMA((2, 10)),
            ],
            compiler_params=pltpu.CompilerParams(
                collective_id=0, has_side_effects=True, vmem_limit_bytes=56 * 2**20
            ),
        )(
            queries.reshape(big),
            out_grad.reshape(big),
            key_vectors.reshape(2, BLK, width),
            value_vectors.reshape(2, BLK, width),
        )
        place = pl.BlockSpec(memory_space=pl.ANY)
        attention, query_grad, key_grad, value_grad = pl.pallas_call(
            hand_over,
            out_shape=shapes,
            in_specs=[place] * 4,
            out_specs=[place] * 4,
            scratch_shapes=[pltpu.SemaphoreType.DMA((4,))],
        )(*results)
        return (
            attention.reshape(queries.shape),
            query_grad.reshape(queries.shape),
            key_grad,
            value_grad,
        )

    tokens = P(("ctxa", "ctxb"), None)
    rows = P(("ctxa", "ctxb"), None, None)
    return jax.shard_map(
        body,
        mesh=mesh,
        in_specs=(rows, tokens, tokens, rows),
        out_specs=(rows, rows, tokens, tokens),
        check_vma=False,
    )
```

```python
import functools

import jax
import jax.numpy as jnp
from jax import lax
from jax.experimental import pallas as pl
from jax.experimental.pallas import tpu as pltpu
from jax.sharding import PartitionSpec as P

BLK = 128
F32 = jnp.float32
BF16 = jnp.bfloat16
MESH = pl.DeviceIdType.MESH
NEG = -1e30
NT = (((1,), (1,)), ((), ()))
NN = (((1,), (0,)), ((), ()))

DISTS = (1, 2, 3, 4, 8, 16, 32, 64, 128, 256)
SLOT = {d: i for i, d in enumerate(DISTS)}
PAIRS = ((8, 16), (64, 32), (128, 256))
OWN = 4
GROUPS = 8


def dot(a, b, dims):
    return lax.dot_general(a, b, dims, preferred_element_type=F32)


def kernel(
    inner, total, q, do, k, v, out, dq, dk, dv,
    win, far, score, prob, top, inv, dlow, qt, dt, delta, term, got, own,
    fsend, frecv, bsend, brecv,
):
    me = lax.axis_index("ctxa") * inner + lax.axis_index("ctxb")
    core = (me // inner) % 2
    scale = 1.0 / BLK**0.5
    unit = scale * 1.4426950408889634

    def place(delta_):
        return ((me + delta_) // inner, (me + delta_) % inner)

    mate = inner * (1 - 2 * core)

    def exists(delta_):
        return (me + delta_ >= 0) & (me + delta_ < total)

    barrier = pltpu.get_barrier_semaphore()
    count = jnp.int32(1)
    pl.semaphore_signal(barrier, inc=1, device_id=place(mate), device_id_type=MESH)
    for step in (2, -2, 128, -128, 64, -64, 1, -1, 8, -8, 16, -16):
        ok = exists(step)

        @pl.when(ok)
        def _(step=step):
            pl.semaphore_signal(barrier, inc=1, device_id=place(step), device_id_type=MESH)

        count = count + ok.astype(jnp.int32)
    pl.semaphore_wait(barrier, count)

    def held(kind, dist):
        if dist == 0:
            return k if kind == 0 else v
        if dist <= 4:
            return win.at[kind, dist - 1]
        for i, pair in enumerate(PAIRS):
            if dist in pair:
                return far.at[kind, i, :, pair.index(dist)]

    forward = [
        (0, 2, 2), (0, 128, 128), (0, 64, 64), (0, 1, 1), (0, 8, 8), (0, 16, 16), (0, 32, 32),
        (2, 2, 4), (2, 1, 3), (128, 128, 256), (64, -32, 32),
    ]

    def forward_ok(item):
        source, step, _ = item
        ok = (me - source >= 0) & exists(step)
        if step == 32:
            ok = core == 0
        if step == -32:
            ok = ok & (core == 1)
        return ok

    def forward_copy(kind, i):
        source, step, target = forward[i]
        return pltpu.make_async_remote_copy(
            src_ref=held(kind, source),
            dst_ref=held(kind, target),
            send_sem=fsend.at[kind, i],
            recv_sem=frecv.at[kind, SLOT[target]],
            device_id=place(step),
            device_id_type=MESH,
        )

    def pass_on(kind, dist):
        for i, item in enumerate(forward):
            if item[0] == dist:

                @pl.when(forward_ok(item))
                def _(i=i):
                    forward_copy(kind, i).start()

    def arrive(kind, dist):
        i = [item[2] for item in forward].index(dist)

        @pl.when(me >= dist)
        def _():
            forward_copy(kind, i).wait_recv()

        pass_on(kind, dist)

    pass_on(0, 0)

    for dist in DISTS:

        @pl.when(me < dist)
        def _(dist=dist):
            for kind in range(2):
                ref = held(kind, dist)
                ref[...] = jnp.zeros(ref.shape, BF16)

    def operand(kind, group, b):
        if group == OWN:
            value = (k if kind == 0 else v)[...]
        elif group < OWN:
            value = win[kind, group]
        else:
            value = far[kind, group - OWN - 1, b]
        return value.reshape(2 * BLK, BLK)

    def scores(group):
        for b in range(2):
            keys = operand(0, group, b)
            for c in range(4):
                rows = pl.ds(c * 256, 256)
                s = dot(q[b, rows, :], keys, NT) * unit
                if group == OWN or group == 3:
                    tok = b * BLK + (c * 256 + lax.broadcasted_iota(jnp.int32, (256, 256), 0)) // 8
                    col = lax.broadcasted_iota(jnp.int32, (256, 256), 1)
                    seen = col <= tok if group == OWN else (col > tok) & (me >= 4)
                    s = jnp.where(seen, s, NEG)
                    s0, s1 = s[:, :BLK], s[:, BLK:]
                else:
                    pair = (group + 1,) * 2 if group < OWN else PAIRS[group - OWN - 1]
                    s0 = jnp.where(me >= pair[0], s[:, :BLK], NEG)
                    s1 = jnp.where(me >= pair[1], s[:, BLK:], NEG)
                score[b, group, rows, :BLK] = s0
                score[b, group, rows, BLK:] = s1
                most = jnp.maximum(s0, s1)
                if group != OWN:
                    most = jnp.maximum(most, top[b, rows, :])
                top[b, rows, :] = most

    for b in range(2):
        for c in range(8):
            qt[b, :, c * BLK : (c + 1) * BLK] = q[b, c * BLK : (c + 1) * BLK, :].T
    scores(OWN)
    for dist in (2, 128, 64):
        arrive(0, dist)
    pass_on(1, 0)
    arrive(0, 1)
    scores(0)
    scores(1)
    for dist in (8, 16):
        arrive(0, dist)
    scores(5)
    for dist in (2, 128, 64):
        arrive(1, dist)
    arrive(0, 3)
    scores(2)
    arrive(0, 32)
    scores(6)
    arrive(0, 4)
    scores(3)
    arrive(0, 256)
    scores(7)

    def soften(i, _):
        b = i // 8
        start = pl.multiple_of((i % 8) * BLK, BLK)
        rows = pl.ds(start, BLK)
        most = jnp.max(top[b, rows, :], axis=1, keepdims=True)
        most = jnp.broadcast_to(most, (BLK, BLK))
        sums = [jnp.zeros((BLK, BLK), F32)] * 2
        for group in range(GROUPS):
            for h in range(2):
                lanes = slice(h * BLK, (h + 1) * BLK)
                e = jnp.exp2(score[b, group, rows, lanes] - most)
                sums[h] = sums[h] + e
                prob[b, group, rows, lanes] = e.astype(BF16)
        part = 1.0 / jnp.sum(sums[0] + sums[1], axis=1, keepdims=True)
        part = jnp.broadcast_to(part, (BLK, BLK))
        inv[b, rows, :] = part
        low = (do[b, rows, :].astype(F32) * part).astype(BF16)
        dlow[b, rows, :] = low
        dt[b, :, rows] = low.T
        return 0

    lax.fori_loop(0, 16, soften, 0, unroll=4)

    back = [
        (4, -4, ()), (3, -1, ()), (256, -256, ()), (128, -128, ()), (32, 0, ()), (16, -16, ()),
        (8, -8, ()), (1, -1, ()), (2, -2, (3,)), (64, -64, (32,)),
    ]
    back_index = {item[0]: i for i, item in enumerate(back)}
    back_step = {item[0]: -item[1] for item in back}

    def back_copy(kind, dist):
        i = back_index[dist]
        step = back[i][1] if dist != 32 else mate
        return pltpu.make_async_remote_copy(
            src_ref=term.at[kind, SLOT[dist]],
            dst_ref=got.at[kind, SLOT[dist]],
            send_sem=bsend.at[kind, i],
            recv_sem=brecv.at[kind, SLOT[dist]],
            device_id=place(step),
            device_id_type=MESH,
        )

    def send_back(kind, dist):
        mine = SLOT[dist]
        for other in back[back_index[dist]][2]:
            if other == 32:
                ok = (me >= dist) & (core == 1)
            else:
                ok = (me >= dist) & exists(back_step[other])

            @pl.when(ok)
            def _(other=other):
                back_copy(kind, other).wait_recv()
                term[kind, mine] = (
                    term[kind, mine].astype(F32) + got[kind, SLOT[other]].astype(F32)
                ).astype(BF16)

        @pl.when(me >= dist)
        def _():
            back_copy(kind, dist).start()

    def reduce_rows(kind, group, left, factor):
        if group <= OWN:
            r = dot(left[0], prob[0, group], NN) + dot(left[1], prob[1, group], NN)
            if group == OWN:
                own[kind] = r * factor
            else:
                term[kind, group] = (r * factor).astype(BF16)
        else:
            pair = PAIRS[group - OWN - 1]
            for b in range(2):
                r = (dot(left[b], prob[b, group], NN) * factor).astype(BF16)
                for h in range(2):
                    term[kind, SLOT[pair[h]], :, b * BLK : (b + 1) * BLK] = r[
                        :, h * BLK : (h + 1) * BLK
                    ]

    order = (
        (3, (4,)), (2, (3,)), (7, (256, 128)), (1, ()), (6, (32,)), (5, (16, 8)), (0, (1,)),
        (OWN, ()),
    )
    for group, dists in order:
        reduce_rows(1, group, dt, 1.0)
        for dist in dists:
            send_back(1, dist)
    for dist in (1, 8, 16, 3, 4, 32, 256):
        arrive(1, dist)

    def attend(i, _):
        b = i // 4
        rows = pl.ds(pl.multiple_of((i % 4) * 256, 256), 256)
        acc = dot(prob[b, 0, rows, :], operand(1, 0, b), NN)
        for group in range(1, GROUPS):
            acc = acc + dot(prob[b, group, rows, :], operand(1, group, b), NN)
        low = (acc * inv[b, rows, :]).astype(BF16)
        out[b, rows, :] = low
        d = jnp.sum(dlow[b, rows, :].astype(F32) * low.astype(F32), axis=1, keepdims=True)
        delta[b, rows, :] = jnp.broadcast_to(d, (256, BLK))
        return 0

    lax.fori_loop(0, 8, attend, 0, unroll=4)

    def score_grads(group):
        for b in range(2):
            values = operand(1, group, b)
            for c in range(4):
                rows = pl.ds(c * 256, 256)
                dp = dot(dlow[b, rows, :], values, NT)
                d = delta[b, rows, :]
                for h in range(2):
                    lanes = slice(h * BLK, (h + 1) * BLK)
                    p = prob[b, group, rows, lanes].astype(F32)
                    prob[b, group, rows, lanes] = (p * (dp[:, lanes] - d)).astype(BF16)
        reduce_rows(0, group, qt, scale)

    for group, dists in order:
        score_grads(group)
        for dist in dists:
            send_back(0, dist)
        if group == 7:
            send_back(1, 2)
            send_back(1, 64)
        if group == 5:
            send_back(0, 2)
        if group == 0:
            send_back(0, 64)

    def query_grads(i, _):
        b = i // 4
        rows = pl.ds(pl.multiple_of((i % 4) * 256, 256), 256)
        acc = dot(prob[b, 0, rows, :], operand(0, 0, b), NN)
        for group in range(1, GROUPS):
            acc = acc + dot(prob[b, group, rows, :], operand(0, group, b), NN)
        dq[b, rows, :] = (acc * scale).astype(BF16)
        return 0

    lax.fori_loop(0, 8, query_grads, 0, unroll=4)

    for kind, result in ((1, dv), (0, dk)):
        for dist in (4, 256, 128, 8, 16, 1, 2, 64, 32):
            ok = (core == 0) if dist == 32 else exists(dist)

            @pl.when(ok)
            def _(kind=kind, dist=dist):
                back_copy(kind, dist).wait_recv()
                own[kind] = own[kind] + got[kind, SLOT[dist]].astype(F32)

        result[...] = own[kind].T.astype(BF16)

    for kind in range(2):
        for i, item in enumerate(forward):

            @pl.when(forward_ok(item))
            def _(kind=kind, i=i):
                forward_copy(kind, i).wait_send()

        for dist in DISTS:

            @pl.when(me >= dist)
            def _(kind=kind, dist=dist):
                back_copy(kind, dist).wait_send()


def hand_over(*refs):
    copies = [pltpu.make_async_copy(refs[i], refs[4 + i], refs[8].at[i]) for i in range(4)]
    for copy in copies:
        copy.start()
    for copy in copies:
        copy.wait()


def solution(mesh):
    inner = mesh.shape["ctxb"]
    total = mesh.shape["ctxa"] * inner

    def body(queries, key_vectors, value_vectors, out_grad):
        toks, heads, width = queries.shape
        rows = toks * heads // 2
        big = (2, rows, width)
        vmem = pl.BlockSpec(memory_space=pltpu.VMEM)
        shapes = (
            jax.ShapeDtypeStruct(big, BF16),
            jax.ShapeDtypeStruct(big, BF16),
            jax.ShapeDtypeStruct((toks, width), BF16),
            jax.ShapeDtypeStruct((toks, width), BF16),
        )
        results = pl.pallas_call(
            functools.partial(kernel, inner, total),
            out_shape=shapes,
            in_specs=[vmem] * 4,
            out_specs=[vmem] * 4,
            scratch_shapes=[
                pltpu.VMEM((2, 4, 2, BLK, width), BF16),
                pltpu.VMEM((2, 3, 2, 2, BLK, width), BF16),
                pltpu.VMEM((2, GROUPS, rows, 2 * BLK), F32),
                pltpu.VMEM((2, GROUPS, rows, 2 * BLK), BF16),
                pltpu.VMEM(big, F32),
                pltpu.VMEM(big, F32),
                pltpu.VMEM(big, BF16),
                pltpu.VMEM((2, width, rows), BF16),
                pltpu.VMEM((2, width, rows), BF16),
                pltpu.VMEM(big, F32),
                pltpu.VMEM((2, 10, width, 2 * BLK), BF16),
                pltpu.VMEM((2, 10, width, 2 * BLK), BF16),
                pltpu.VMEM((2, width, 2 * BLK), F32),
                pltpu.SemaphoreType.DMA((2, 11)),
                pltpu.SemaphoreType.DMA((2, 10)),
                pltpu.SemaphoreType.DMA((2, 10)),
                pltpu.SemaphoreType.DMA((2, 10)),
            ],
            compiler_params=pltpu.CompilerParams(
                collective_id=0, has_side_effects=True, vmem_limit_bytes=56 * 2**20
            ),
        )(
            queries.reshape(big),
            out_grad.reshape(big),
            key_vectors.reshape(2, BLK, width),
            value_vectors.reshape(2, BLK, width),
        )
        place = pl.BlockSpec(memory_space=pl.ANY)
        attention, query_grad, key_grad, value_grad = pl.pallas_call(
            hand_over,
            out_shape=shapes,
            in_specs=[vmem] * 4,
            out_specs=[place] * 4,
            scratch_shapes=[pltpu.SemaphoreType.DMA((4,))],
        )(*results)
        return (
            attention.reshape(queries.shape),
            query_grad.reshape(queries.shape),
            key_grad,
            value_grad,
        )

    tokens = P(("ctxa", "ctxb"), None)
    rows = P(("ctxa", "ctxb"), None, None)
    return jax.shard_map(
        body,
        mesh=mesh,
        in_specs=(rows, tokens, tokens, rows),
        out_specs=(rows, rows, tokens, tokens),
        check_vma=False,
    )
```

```python
import functools

import jax
import jax.numpy as jnp
from jax import lax
from jax.experimental import pallas as pl
from jax.experimental.pallas import tpu as pltpu
from jax.sharding import PartitionSpec as P

BLK = 128
F32 = jnp.float32
BF16 = jnp.bfloat16
MESH = pl.DeviceIdType.MESH
NEG = -1e30
NT = (((1,), (1,)), ((), ()))
NN = (((1,), (0,)), ((), ()))

DISTS = (1, 2, 3, 4, 8, 16, 32, 64, 128, 256)
SLOT = {d: i for i, d in enumerate(DISTS)}
PAIRS = ((8, 16), (64, 32), (128, 256))
OWN = 4
GROUPS = 8


def dot(a, b, dims):
    return lax.dot_general(a, b, dims, preferred_element_type=F32)


def kernel(
    inner, total, q_in, do_in, k, v, out, dq, dk, dv,
    q, do, win, far, score, prob, top, inv, dlow, qt, dt, delta, term, got, own,
    load, fsend, frecv, bsend, brecv,
):
    me = lax.axis_index("ctxa") * inner + lax.axis_index("ctxb")
    core = (me // inner) % 2
    scale = 1.0 / BLK**0.5
    unit = scale * 1.4426950408889634

    def place(delta_):
        return ((me + delta_) // inner, (me + delta_) % inner)

    mate = inner * (1 - 2 * core)

    def exists(delta_):
        return (me + delta_ >= 0) & (me + delta_ < total)

    barrier = pltpu.get_barrier_semaphore()
    count = jnp.int32(1)
    pl.semaphore_signal(barrier, inc=1, device_id=place(mate), device_id_type=MESH)
    for step in (2, -2, 128, -128, 64, -64, 1, -1, 8, -8, 16, -16):
        ok = exists(step)

        @pl.when(ok)
        def _(step=step):
            pl.semaphore_signal(barrier, inc=1, device_id=place(step), device_id_type=MESH)

        count = count + ok.astype(jnp.int32)
    loads = [
        pltpu.make_async_copy(q_in, q, load.at[0]),
        pltpu.make_async_copy(do_in, do, load.at[1]),
    ]
    for copy in loads:
        copy.start()
    pl.semaphore_wait(barrier, count)

    def held(kind, dist, half=None):
        if dist == 0:
            ref = k if kind == 0 else v
            return ref if half is None else ref.at[half]
        if dist <= 4:
            return win.at[kind, dist - 1] if half is None else win.at[kind, dist - 1, half]
        for i, pair in enumerate(PAIRS):
            if dist in pair:
                return far.at[kind, i, slice(None) if half is None else half, pair.index(dist)]

    forward = [
        (0, 2, 2, 0), (0, 128, 128, 0), (0, 2, 2, 1), (0, 128, 128, 1), (0, 64, 64, None),
        (0, 1, 1, None), (0, 8, 8, None), (0, 16, 16, None), (0, 32, 32, None),
        (2, 2, 4, 0), (2, 1, 3, 0), (128, 128, 256, 0), (2, 2, 4, 1), (2, 1, 3, 1),
        (128, 128, 256, 1), (64, -32, 32, None),
    ]

    def forward_ok(item):
        source, step = item[:2]
        ok = (me - source >= 0) & exists(step)
        if step == 32:
            ok = core == 0
        if step == -32:
            ok = ok & (core == 1)
        return ok

    def forward_copy(kind, i):
        source, step, target, half = forward[i]
        return pltpu.make_async_remote_copy(
            src_ref=held(kind, source, half),
            dst_ref=held(kind, target, half),
            send_sem=fsend.at[kind, i],
            recv_sem=frecv.at[kind, SLOT[target], half or 0],
            device_id=place(step),
            device_id_type=MESH,
        )

    def pass_on(kind, dist, halves):
        for i, item in enumerate(forward):
            if item[0] == dist and item[3] in halves:

                @pl.when(forward_ok(item))
                def _(i=i):
                    forward_copy(kind, i).start()

    def arrive(kind, dist, halves=(None, 0, 1)):
        for half in halves:
            into = [i for i, item in enumerate(forward) if item[2:] == (dist, half)]
            if into:
                @pl.when(me >= dist)
                def _(i=into[0]):
                    forward_copy(kind, i).wait_recv()

                pass_on(kind, dist, (half,))

    pass_on(0, 0, (None, 0, 1))

    for dist in DISTS:

        @pl.when(me < dist)
        def _(dist=dist):
            for kind in range(2):
                ref = held(kind, dist)
                ref[...] = jnp.zeros(ref.shape, BF16)

    def operand(kind, group, b):
        if group == OWN:
            value = (k if kind == 0 else v)[...]
        elif group < OWN:
            value = win[kind, group]
        else:
            value = far[kind, group - OWN - 1, b]
        return value.reshape(2 * BLK, BLK)

    def scores(group):
        for b in range(2):
            keys = operand(0, group, b)
            for c in range(4):
                rows = pl.ds(c * 256, 256)
                s = dot(q[b, rows, :], keys, NT) * unit
                if group == OWN or group == 3:
                    tok = b * BLK + (c * 256 + lax.broadcasted_iota(jnp.int32, (256, 256), 0)) // 8
                    col = lax.broadcasted_iota(jnp.int32, (256, 256), 1)
                    seen = col <= tok if group == OWN else (col > tok) & (me >= 4)
                    s = jnp.where(seen, s, NEG)
                    s0, s1 = s[:, :BLK], s[:, BLK:]
                else:
                    pair = (group + 1,) * 2 if group < OWN else PAIRS[group - OWN - 1]
                    s0 = jnp.where(me >= pair[0], s[:, :BLK], NEG)
                    s1 = jnp.where(me >= pair[1], s[:, BLK:], NEG)
                score[b, group, rows, :BLK] = s0
                score[b, group, rows, BLK:] = s1
                most = jnp.maximum(s0, s1)
                if group != OWN:
                    most = jnp.maximum(most, top[b, rows, :])
                top[b, rows, :] = most

    loads[0].wait()
    for b in range(2):
        for c in range(8):
            qt[b, :, c * BLK : (c + 1) * BLK] = q[b, c * BLK : (c + 1) * BLK, :].T
    scores(OWN)
    for half in (0, 1):
        for dist in (2, 128):
            arrive(0, dist, (half,))
    arrive(0, 64)
    pass_on(1, 0, (None, 0, 1))
    arrive(0, 1)
    scores(0)
    scores(1)
    for dist in (8, 16):
        arrive(0, dist)
    scores(5)
    for half in (0, 1):
        for dist in (2, 128):
            arrive(1, dist, (half,))
    arrive(1, 64)
    arrive(0, 3)
    scores(2)
    arrive(0, 32)
    scores(6)
    arrive(0, 4)
    scores(3)
    arrive(0, 256)
    scores(7)

    def soften(i, _):
        b = i // 8
        start = pl.multiple_of((i % 8) * BLK, BLK)
        rows = pl.ds(start, BLK)
        most = jnp.max(top[b, rows, :], axis=1, keepdims=True)
        most = jnp.broadcast_to(most, (BLK, BLK))
        sums = [jnp.zeros((BLK, BLK), F32)] * 2
        for group in range(GROUPS):
            for h in range(2):
                lanes = slice(h * BLK, (h + 1) * BLK)
                e = jnp.exp2(score[b, group, rows, lanes] - most)
                sums[h] = sums[h] + e
                prob[b, group, rows, lanes] = e.astype(BF16)
        part = 1.0 / jnp.sum(sums[0] + sums[1], axis=1, keepdims=True)
        part = jnp.broadcast_to(part, (BLK, BLK))
        inv[b, rows, :] = part
        low = (do[b, rows, :].astype(F32) * part).astype(BF16)
        dlow[b, rows, :] = low
        dt[b, :, rows] = low.T
        return 0

    loads[1].wait()
    lax.fori_loop(0, 16, soften, 0, unroll=4)

    back = [
        (4, -4, ()), (3, -1, ()), (256, -256, ()), (128, -128, ()), (32, 0, ()), (16, -16, ()),
        (8, -8, ()), (1, -1, ()), (2, -2, (3,)), (64, -64, (32,)),
    ]
    back_index = {item[0]: i for i, item in enumerate(back)}
    back_step = {item[0]: -item[1] for item in back}

    def back_copy(kind, dist):
        i = back_index[dist]
        step = back[i][1] if dist != 32 else mate
        return pltpu.make_async_remote_copy(
            src_ref=term.at[kind, SLOT[dist]],
            dst_ref=got.at[kind, SLOT[dist]],
            send_sem=bsend.at[kind, i],
            recv_sem=brecv.at[kind, SLOT[dist]],
            device_id=place(step),
            device_id_type=MESH,
        )

    def send_back(kind, dist):
        mine = SLOT[dist]
        for other in back[back_index[dist]][2]:
            if other == 32:
                ok = (me >= dist) & (core == 1)
            else:
                ok = (me >= dist) & exists(back_step[other])

            @pl.when(ok)
            def _(other=other):
                back_copy(kind, other).wait_recv()
                term[kind, mine] = (
                    term[kind, mine].astype(F32) + got[kind, SLOT[other]].astype(F32)
                ).astype(BF16)

        @pl.when(me >= dist)
        def _():
            back_copy(kind, dist).start()

    def reduce_rows(kind, group, left, factor):
        if group <= OWN:
            r = dot(left[0], prob[0, group], NN) + dot(left[1], prob[1, group], NN)
            if group == OWN:
                own[kind] = r * factor
            else:
                term[kind, group] = (r * factor).astype(BF16)
        else:
            pair = PAIRS[group - OWN - 1]
            for b in range(2):
                r = (dot(left[b], prob[b, group], NN) * factor).astype(BF16)
                for h in range(2):
                    term[kind, SLOT[pair[h]], :, b * BLK : (b + 1) * BLK] = r[
                        :, h * BLK : (h + 1) * BLK
                    ]

    order = (
        (3, (4,)), (2, (3,)), (7, (256, 128)), (1, ()), (6, (32,)), (5, (16, 8)), (0, (1,)),
        (OWN, ()),
    )
    for group, dists in order:
        reduce_rows(1, group, dt, 1.0)
        for dist in dists:
            send_back(1, dist)
    for dist in (1, 8, 16, 3, 4, 32, 256):
        arrive(1, dist)

    def attend(i, _):
        b = i // 4
        rows = pl.ds(pl.multiple_of((i % 4) * 256, 256), 256)
        acc = dot(prob[b, 0, rows, :], operand(1, 0, b), NN)
        for group in range(1, GROUPS):
            acc = acc + dot(prob[b, group, rows, :], operand(1, group, b), NN)
        low = (acc * inv[b, rows, :]).astype(BF16)
        out[b, rows, :] = low
        d = jnp.sum(dlow[b, rows, :].astype(F32) * low.astype(F32), axis=1, keepdims=True)
        delta[b, rows, :] = jnp.broadcast_to(d, (256, BLK))
        return 0

    lax.fori_loop(0, 8, attend, 0, unroll=4)

    def score_grads(group):
        for b in range(2):
            values = operand(1, group, b)
            for c in range(4):
                rows = pl.ds(c * 256, 256)
                dp = dot(dlow[b, rows, :], values, NT)
                d = delta[b, rows, :]
                for h in range(2):
                    lanes = slice(h * BLK, (h + 1) * BLK)
                    p = prob[b, group, rows, lanes].astype(F32)
                    prob[b, group, rows, lanes] = (p * (dp[:, lanes] - d)).astype(BF16)
        reduce_rows(0, group, qt, scale)

    for group, dists in order:
        score_grads(group)
        for dist in dists:
            send_back(0, dist)
        if group == 7:
            send_back(1, 2)
            send_back(1, 64)
        if group == 5:
            send_back(0, 2)
        if group == 0:
            send_back(0, 64)

    def query_grads(i, _):
        b = i // 4
        rows = pl.ds(pl.multiple_of((i % 4) * 256, 256), 256)
        acc = dot(prob[b, 0, rows, :], operand(0, 0, b), NN)
        for group in range(1, GROUPS):
            acc = acc + dot(prob[b, group, rows, :], operand(0, group, b), NN)
        dq[b, rows, :] = (acc * scale).astype(BF16)
        return 0

    lax.fori_loop(0, 8, query_grads, 0, unroll=4)

    for kind, result in ((1, dv), (0, dk)):
        for dist in (4, 256, 128, 8, 16, 1, 2, 64, 32):
            ok = (core == 0) if dist == 32 else exists(dist)

            @pl.when(ok)
            def _(kind=kind, dist=dist):
                back_copy(kind, dist).wait_recv()
                own[kind] = own[kind] + got[kind, SLOT[dist]].astype(F32)

        result[...] = own[kind].T.astype(BF16)

    for kind in range(2):
        for i, item in enumerate(forward):

            @pl.when(forward_ok(item))
            def _(kind=kind, i=i):
                forward_copy(kind, i).wait_send()

        for dist in DISTS:

            @pl.when(me >= dist)
            def _(kind=kind, dist=dist):
                back_copy(kind, dist).wait_send()


def hand_over(*refs):
    copies = [pltpu.make_async_copy(refs[i], refs[4 + i], refs[8].at[i]) for i in range(4)]
    for copy in copies:
        copy.start()
    for copy in copies:
        copy.wait()


def solution(mesh):
    inner = mesh.shape["ctxb"]
    total = mesh.shape["ctxa"] * inner

    def body(queries, key_vectors, value_vectors, out_grad):
        toks, heads, width = queries.shape
        rows = toks * heads // 2
        big = (2, rows, width)
        vmem = pl.BlockSpec(memory_space=pltpu.VMEM)
        place = pl.BlockSpec(memory_space=pl.ANY)
        shapes = (
            jax.ShapeDtypeStruct(big, BF16),
            jax.ShapeDtypeStruct(big, BF16),
            jax.ShapeDtypeStruct((toks, width), BF16),
            jax.ShapeDtypeStruct((toks, width), BF16),
        )
        results = pl.pallas_call(
            functools.partial(kernel, inner, total),
            out_shape=shapes,
            in_specs=[place, place, vmem, vmem],
            out_specs=[vmem] * 4,
            scratch_shapes=[
                pltpu.VMEM(big, BF16),
                pltpu.VMEM(big, BF16),
                pltpu.VMEM((2, 4, 2, BLK, width), BF16),
                pltpu.VMEM((2, 3, 2, 2, BLK, width), BF16),
                pltpu.VMEM((2, GROUPS, rows, 2 * BLK), F32),
                pltpu.VMEM((2, GROUPS, rows, 2 * BLK), BF16),
                pltpu.VMEM(big, F32),
                pltpu.VMEM(big, F32),
                pltpu.VMEM(big, BF16),
                pltpu.VMEM((2, width, rows), BF16),
                pltpu.VMEM((2, width, rows), BF16),
                pltpu.VMEM(big, F32),
                pltpu.VMEM((2, 10, width, 2 * BLK), BF16),
                pltpu.VMEM((2, 10, width, 2 * BLK), BF16),
                pltpu.VMEM((2, width, 2 * BLK), F32),
                pltpu.SemaphoreType.DMA((2,)),
                pltpu.SemaphoreType.DMA((2, 16)),
                pltpu.SemaphoreType.DMA((2, 10, 2)),
                pltpu.SemaphoreType.DMA((2, 10)),
                pltpu.SemaphoreType.DMA((2, 10)),
            ],
            compiler_params=pltpu.CompilerParams(
                collective_id=0, has_side_effects=True, vmem_limit_bytes=56 * 2**20
            ),
        )(
            queries.reshape(big),
            out_grad.reshape(big),
            key_vectors.reshape(2, BLK, width),
            value_vectors.reshape(2, BLK, width),
        )
        attention, query_grad, key_grad, value_grad = pl.pallas_call(
            hand_over,
            out_shape=shapes,
            in_specs=[vmem] * 4,
            out_specs=[place] * 4,
            scratch_shapes=[pltpu.SemaphoreType.DMA((4,))],
        )(*results)
        return (
            attention.reshape(queries.shape),
            query_grad.reshape(queries.shape),
            key_grad,
            value_grad,
        )

    tokens = P(("ctxa", "ctxb"), None)
    rows = P(("ctxa", "ctxb"), None, None)
    return jax.shard_map(
        body,
        mesh=mesh,
        in_specs=(rows, tokens, tokens, rows),
        out_specs=(rows, rows, tokens, tokens),
        check_vma=False,
    )
```

```python
import functools

import jax
import jax.numpy as jnp
from jax import lax
from jax.experimental import pallas as pl
from jax.experimental.pallas import tpu as pltpu
from jax.sharding import PartitionSpec as P

BLK = 128
F32 = jnp.float32
BF16 = jnp.bfloat16
MESH = pl.DeviceIdType.MESH
NEG = -1e30
NT = (((1,), (1,)), ((), ()))
NN = (((1,), (0,)), ((), ()))

DISTS = (1, 2, 3, 4, 8, 16, 32, 64, 128, 256)
SLOT = {d: i for i, d in enumerate(DISTS)}
PAIRS = ((8, 16), (64, 32), (128, 256))
OWN = 4
GROUPS = 8
EARLY = (OWN, 0, 1, 5)


def dot(a, b, dims):
    return lax.dot_general(a, b, dims, preferred_element_type=F32)


def kernel(
    inner, total, q_in, do_in, k, v, out, dq, dk, dv,
    q, do, win, far, score, prob, top, first, sums, inv, dlow, qt, dt, delta, term, got, own,
    load, fsend, frecv, bsend, brecv,
):
    me = lax.axis_index("ctxa") * inner + lax.axis_index("ctxb")
    core = (me // inner) % 2
    scale = 1.0 / BLK**0.5
    unit = scale * 1.4426950408889634

    def place(delta_):
        return ((me + delta_) // inner, (me + delta_) % inner)

    mate = inner * (1 - 2 * core)

    def exists(delta_):
        return (me + delta_ >= 0) & (me + delta_ < total)

    barrier = pltpu.get_barrier_semaphore()
    count = jnp.int32(1)
    pl.semaphore_signal(barrier, inc=1, device_id=place(mate), device_id_type=MESH)
    for step in (2, -2, 128, -128, 64, -64, 1, -1, 8, -8, 16, -16):
        ok = exists(step)

        @pl.when(ok)
        def _(step=step):
            pl.semaphore_signal(barrier, inc=1, device_id=place(step), device_id_type=MESH)

        count = count + ok.astype(jnp.int32)
    loads = [
        pltpu.make_async_copy(q_in, q, load.at[0]),
        pltpu.make_async_copy(do_in, do, load.at[1]),
    ]
    for copy in loads:
        copy.start()
    pl.semaphore_wait(barrier, count)

    def held(kind, dist, half=None):
        if dist == 0:
            ref = k if kind == 0 else v
            return ref if half is None else ref.at[half]
        if dist <= 4:
            return win.at[kind, dist - 1] if half is None else win.at[kind, dist - 1, half]
        for i, pair in enumerate(PAIRS):
            if dist in pair:
                return far.at[kind, i, slice(None) if half is None else half, pair.index(dist)]

    forward = [
        (0, 2, 2, 0), (0, 128, 128, 0), (0, 2, 2, 1), (0, 128, 128, 1), (0, 64, 64, None),
        (0, 1, 1, None), (0, 8, 8, None), (0, 16, 16, None), (0, 32, 32, None),
        (2, 2, 4, 0), (2, 1, 3, 0), (128, 128, 256, 0), (2, 2, 4, 1), (2, 1, 3, 1),
        (128, 128, 256, 1), (64, -32, 32, None),
    ]

    def forward_ok(item):
        source, step = item[:2]
        ok = (me - source >= 0) & exists(step)
        if step == 32:
            ok = core == 0
        if step == -32:
            ok = ok & (core == 1)
        return ok

    def forward_copy(kind, i):
        source, step, target, half = forward[i]
        return pltpu.make_async_remote_copy(
            src_ref=held(kind, source, half),
            dst_ref=held(kind, target, half),
            send_sem=fsend.at[kind, i],
            recv_sem=frecv.at[kind, SLOT[target], half or 0],
            device_id=place(step),
            device_id_type=MESH,
        )

    def pass_on(kind, dist, halves):
        for i, item in enumerate(forward):
            if item[0] == dist and item[3] in halves:

                @pl.when(forward_ok(item))
                def _(i=i):
                    forward_copy(kind, i).start()

    def arrive(kind, dist, halves=(None, 0, 1)):
        for half in halves:
            into = [i for i, item in enumerate(forward) if item[2:] == (dist, half)]
            if into:
                @pl.when(me >= dist)
                def _(i=into[0]):
                    forward_copy(kind, i).wait_recv()

                pass_on(kind, dist, (half,))

    pass_on(0, 0, (None, 0, 1))

    for dist in DISTS:

        @pl.when(me < dist)
        def _(dist=dist):
            for kind in range(2):
                ref = held(kind, dist)
                ref[...] = jnp.zeros(ref.shape, BF16)

    def operand(kind, group, b):
        if group == OWN:
            value = (k if kind == 0 else v)[...]
        elif group < OWN:
            value = win[kind, group]
        else:
            value = far[kind, group - OWN - 1, b]
        return value.reshape(2 * BLK, BLK)

    def exponentials(b, rows, groups, most):
        total_ = [jnp.zeros((BLK, BLK), F32)] * 2
        for group in groups:
            for h in range(2):
                lanes = slice(h * BLK, (h + 1) * BLK)
                e = jnp.exp2(score[b, group, rows, lanes] - most)
                total_[h] = total_[h] + e
                prob[b, group, rows, lanes] = e.astype(BF16)
        return total_[0] + total_[1]

    def row_max(b, rows):
        most = jnp.max(top[b, rows, :], axis=1, keepdims=True)
        return jnp.broadcast_to(most, (BLK, BLK))

    def soften_early(i, _):
        b = i // 8
        rows = pl.ds(pl.multiple_of((i % 8) * BLK, BLK), BLK)
        most = row_max(b, rows)
        first[b, rows, :] = most
        sums[b, rows, :] = exponentials(b, rows, EARLY, most)
        return 0

    def soften(i, _):
        b = i // 8
        rows = pl.ds(pl.multiple_of((i % 8) * BLK, BLK), BLK)
        most = row_max(b, rows)
        shrink = jnp.exp2(first[b, rows, :] - most)
        late = [g for g in range(GROUPS) if g not in EARLY]
        all_ = sums[b, rows, :] * shrink + exponentials(b, rows, late, most)
        part = 1.0 / jnp.sum(all_, axis=1, keepdims=True)
        part = jnp.broadcast_to(part, (BLK, BLK))
        for part_set, weight in enumerate((part * shrink, part)):
            inv[part_set, b, rows, :] = weight
            low = (do[b, rows, :].astype(F32) * weight).astype(BF16)
            dlow[part_set, b, rows, :] = low
            dt[part_set, b, :, rows] = low.T
        return 0

    def set_of(group):
        return 0 if group in EARLY else 1

    def scores(group):
        for b in range(2):
            keys = operand(0, group, b)
            for c in range(4):
                rows = pl.ds(c * 256, 256)
                s = dot(q[b, rows, :], keys, NT) * unit
                if group == OWN or group == 3:
                    tok = b * BLK + (c * 256 + lax.broadcasted_iota(jnp.int32, (256, 256), 0)) // 8
                    col = lax.broadcasted_iota(jnp.int32, (256, 256), 1)
                    seen = col <= tok if group == OWN else (col > tok) & (me >= 4)
                    s = jnp.where(seen, s, NEG)
                    s0, s1 = s[:, :BLK], s[:, BLK:]
                else:
                    pair = (group + 1,) * 2 if group < OWN else PAIRS[group - OWN - 1]
                    s0 = jnp.where(me >= pair[0], s[:, :BLK], NEG)
                    s1 = jnp.where(me >= pair[1], s[:, BLK:], NEG)
                score[b, group, rows, :BLK] = s0
                score[b, group, rows, BLK:] = s1
                most = jnp.maximum(s0, s1)
                if group != OWN:
                    most = jnp.maximum(most, top[b, rows, :])
                top[b, rows, :] = most

    loads[0].wait()
    for b in range(2):
        for c in range(8):
            qt[b, :, c * BLK : (c + 1) * BLK] = q[b, c * BLK : (c + 1) * BLK, :].T
    scores(OWN)
    for half in (0, 1):
        for dist in (2, 128):
            arrive(0, dist, (half,))
    arrive(0, 64)
    pass_on(1, 0, (None, 0, 1))
    arrive(0, 1)
    scores(0)
    scores(1)
    for dist in (8, 16):
        arrive(0, dist)
    scores(5)
    lax.fori_loop(0, 16, soften_early, 0, unroll=4)
    for half in (0, 1):
        for dist in (2, 128):
            arrive(1, dist, (half,))
    arrive(1, 64)
    arrive(0, 3)
    scores(2)
    arrive(0, 32)
    scores(6)
    arrive(0, 4)
    scores(3)
    arrive(0, 256)
    scores(7)

    loads[1].wait()
    lax.fori_loop(0, 16, soften, 0, unroll=4)

    back = [
        (4, -4, ()), (3, -1, ()), (256, -256, ()), (128, -128, ()), (32, 0, ()), (16, -16, ()),
        (8, -8, ()), (1, -1, ()), (2, -2, (3,)), (64, -64, (32,)),
    ]
    back_index = {item[0]: i for i, item in enumerate(back)}
    back_step = {item[0]: -item[1] for item in back}

    def back_copy(kind, dist):
        i = back_index[dist]
        step = back[i][1] if dist != 32 else mate
        return pltpu.make_async_remote_copy(
            src_ref=term.at[kind, SLOT[dist]],
            dst_ref=got.at[kind, SLOT[dist]],
            send_sem=bsend.at[kind, i],
            recv_sem=brecv.at[kind, SLOT[dist]],
            device_id=place(step),
            device_id_type=MESH,
        )

    def send_back(kind, dist):
        mine = SLOT[dist]
        for other in back[back_index[dist]][2]:
            if other == 32:
                ok = (me >= dist) & (core == 1)
            else:
                ok = (me >= dist) & exists(back_step[other])

            @pl.when(ok)
            def _(other=other):
                back_copy(kind, other).wait_recv()
                term[kind, mine] = (
                    term[kind, mine].astype(F32) + got[kind, SLOT[other]].astype(F32)
                ).astype(BF16)

        @pl.when(me >= dist)
        def _():
            back_copy(kind, dist).start()

    def reduce_rows(kind, group, left, factor):
        if group <= OWN:
            r = dot(left[0], prob[0, group], NN) + dot(left[1], prob[1, group], NN)
            if group == OWN:
                own[kind] = r * factor
            else:
                term[kind, group] = (r * factor).astype(BF16)
        else:
            pair = PAIRS[group - OWN - 1]
            for b in range(2):
                r = (dot(left[b], prob[b, group], NN) * factor).astype(BF16)
                for h in range(2):
                    term[kind, SLOT[pair[h]], :, b * BLK : (b + 1) * BLK] = r[
                        :, h * BLK : (h + 1) * BLK
                    ]

    order = (
        (3, (4,)), (2, (3,)), (7, (256, 128)), (1, ()), (6, (32,)), (5, (16, 8)), (0, (1,)),
        (OWN, ()),
    )
    for group, dists in order:
        reduce_rows(1, group, dt.at[set_of(group)], 1.0)
        for dist in dists:
            send_back(1, dist)
    for dist in (1, 8, 16, 3, 4, 32, 256):
        arrive(1, dist)

    def attend(i, _):
        b = i // 4
        rows = pl.ds(pl.multiple_of((i % 4) * 256, 256), 256)
        acc = [None, None]
        for group in range(GROUPS):
            r = dot(prob[b, group, rows, :], operand(1, group, b), NN)
            n = set_of(group)
            acc[n] = r if acc[n] is None else acc[n] + r
        low = (acc[0] * inv[0, b, rows, :] + acc[1] * inv[1, b, rows, :]).astype(BF16)
        out[b, rows, :] = low
        for n in range(2):
            d = dlow[n, b, rows, :].astype(F32) * low.astype(F32)
            d = jnp.sum(d, axis=1, keepdims=True)
            delta[n, b, rows, :] = jnp.broadcast_to(d, (256, BLK))
        return 0

    lax.fori_loop(0, 8, attend, 0, unroll=4)

    def score_grads(group):
        for b in range(2):
            values = operand(1, group, b)
            for c in range(4):
                rows = pl.ds(c * 256, 256)
                dp = dot(dlow[set_of(group), b, rows, :], values, NT)
                d = delta[set_of(group), b, rows, :]
                for h in range(2):
                    lanes = slice(h * BLK, (h + 1) * BLK)
                    p = prob[b, group, rows, lanes].astype(F32)
                    prob[b, group, rows, lanes] = (p * (dp[:, lanes] - d)).astype(BF16)
        reduce_rows(0, group, qt, scale)

    for group, dists in order:
        score_grads(group)
        for dist in dists:
            send_back(0, dist)
        if group == 7:
            send_back(1, 2)
            send_back(1, 64)
        if group == 5:
            send_back(0, 2)
        if group == 0:
            send_back(0, 64)

    def query_grads(i, _):
        b = i // 4
        rows = pl.ds(pl.multiple_of((i % 4) * 256, 256), 256)
        acc = dot(prob[b, 0, rows, :], operand(0, 0, b), NN)
        for group in range(1, GROUPS):
            acc = acc + dot(prob[b, group, rows, :], operand(0, group, b), NN)
        dq[b, rows, :] = (acc * scale).astype(BF16)
        return 0

    lax.fori_loop(0, 8, query_grads, 0, unroll=4)

    for kind, result in ((1, dv), (0, dk)):
        for dist in (4, 256, 128, 8, 16, 1, 2, 64, 32):
            ok = (core == 0) if dist == 32 else exists(dist)

            @pl.when(ok)
            def _(kind=kind, dist=dist):
                back_copy(kind, dist).wait_recv()
                own[kind] = own[kind] + got[kind, SLOT[dist]].astype(F32)

        result[...] = own[kind].T.astype(BF16)

    for kind in range(2):
        for i, item in enumerate(forward):

            @pl.when(forward_ok(item))
            def _(kind=kind, i=i):
                forward_copy(kind, i).wait_send()

        for dist in DISTS:

            @pl.when(me >= dist)
            def _(kind=kind, dist=dist):
                back_copy(kind, dist).wait_send()


def hand_over(*refs):
    copies = [pltpu.make_async_copy(refs[i], refs[4 + i], refs[8].at[i]) for i in range(4)]
    for copy in copies:
        copy.start()
    for copy in copies:
        copy.wait()


def solution(mesh):
    inner = mesh.shape["ctxb"]
    total = mesh.shape["ctxa"] * inner

    def body(queries, key_vectors, value_vectors, out_grad):
        toks, heads, width = queries.shape
        rows = toks * heads // 2
        big = (2, rows, width)
        vmem = pl.BlockSpec(memory_space=pltpu.VMEM)
        place = pl.BlockSpec(memory_space=pl.ANY)
        shapes = (
            jax.ShapeDtypeStruct(big, BF16),
            jax.ShapeDtypeStruct(big, BF16),
            jax.ShapeDtypeStruct((toks, width), BF16),
            jax.ShapeDtypeStruct((toks, width), BF16),
        )
        results = pl.pallas_call(
            functools.partial(kernel, inner, total),
            out_shape=shapes,
            in_specs=[place, place, vmem, vmem],
            out_specs=[vmem] * 4,
            scratch_shapes=[
                pltpu.VMEM(big, BF16),
                pltpu.VMEM(big, BF16),
                pltpu.VMEM((2, 4, 2, BLK, width), BF16),
                pltpu.VMEM((2, 3, 2, 2, BLK, width), BF16),
                pltpu.VMEM((2, GROUPS, rows, 2 * BLK), F32),
                pltpu.VMEM((2, GROUPS, rows, 2 * BLK), BF16),
                pltpu.VMEM(big, F32),
                pltpu.VMEM(big, F32),
                pltpu.VMEM(big, F32),
                pltpu.VMEM((2, *big), F32),
                pltpu.VMEM((2, *big), BF16),
                pltpu.VMEM((2, width, rows), BF16),
                pltpu.VMEM((2, 2, width, rows), BF16),
                pltpu.VMEM((2, *big), F32),
                pltpu.VMEM((2, 10, width, 2 * BLK), BF16),
                pltpu.VMEM((2, 10, width, 2 * BLK), BF16),
                pltpu.VMEM((2, width, 2 * BLK), F32),
                pltpu.SemaphoreType.DMA((2,)),
                pltpu.SemaphoreType.DMA((2, 16)),
                pltpu.SemaphoreType.DMA((2, 10, 2)),
                pltpu.SemaphoreType.DMA((2, 10)),
                pltpu.SemaphoreType.DMA((2, 10)),
            ],
            compiler_params=pltpu.CompilerParams(
                collective_id=0, has_side_effects=True, vmem_limit_bytes=56 * 2**20
            ),
        )(
            queries.reshape(big),
            out_grad.reshape(big),
            key_vectors.reshape(2, BLK, width),
            value_vectors.reshape(2, BLK, width),
        )
        attention, query_grad, key_grad, value_grad = pl.pallas_call(
            hand_over,
            out_shape=shapes,
            in_specs=[vmem] * 4,
            out_specs=[place] * 4,
            scratch_shapes=[pltpu.SemaphoreType.DMA((4,))],
        )(*results)
        return (
            attention.reshape(queries.shape),
            query_grad.reshape(queries.shape),
            key_grad,
            value_grad,
        )

    tokens = P(("ctxa", "ctxb"), None)
    rows = P(("ctxa", "ctxb"), None, None)
    return jax.shard_map(
        body,
        mesh=mesh,
        in_specs=(rows, tokens, tokens, rows),
        out_specs=(rows, rows, tokens, tokens),
        check_vma=False,
    )
```
